32 devices in a mesh: frame: 8 (over z, x), row: 4 (over y, core).
Axes of the slice: x: 2, y: 2, z: 4, core: 2. Of those that a mesh axis runs over, the one named last changes fastest.
Arguments:
- tokens: bfloat16 [8, 1024, 512], P('frame', 'row'), may hold values from -15 to 15
- norm_spatial: float32 [512], replicated, may hold values from 0.25 to 1.75
- w_spatial: bfloat16 [512, 1536], replicated, may hold values from -10 to 10
- w_spatial_out: bfloat16 [512, 512], replicated, may hold values from -0.25 to 0.25
- norm_temporal: float32 [512], replicated, may hold values from 0.25 to 1.75
- w_temporal: bfloat16 [512, 1536], replicated, may hold values from -10 to 10
- w_temporal_out: bfloat16 [512, 512], replicated, may hold values from -0.25 to 0.25
Outputs:
- mixed: bfloat16 [8, 1024, 512], P('frame', 'row')
The draws below stay inside these ranges and needn't reach their ends.
All inputs are finite; a program needn't handle non-finite values.
Results may differ from the reference program's by a relative error of at most 0.01.
The reference program's roundings to bfloat16 on the way count: a program that leaves them out, or rounds other values in their place, can miss the bound.
Values may be sent and summed in bfloat16 or wider, within the bound.
A program may use at most 64 MiB of HBM per device.

```python
import math
import jax
import jax.numpy as jnp
from jax import lax

D = 512
HEADS = 8
HEAD = 64
CELLS = 1024
FRAMES = 8


def attention_weights(key):
    root = 1.0 / math.sqrt(D)
    query = jnp.clip(jax.random.normal(jax.random.fold_in(key, 1), (D, D), jnp.float32), -6.0, 6.0) * (1.6 * root)
    keys = jnp.clip(jax.random.normal(jax.random.fold_in(key, 2), (D, D), jnp.float32), -6.0, 6.0) * (1.6 * root)
    values = jnp.clip(jax.random.normal(jax.random.fold_in(key, 3), (D, D), jnp.float32), -6.0, 6.0) * root
    return jnp.concatenate([query, keys, values], axis=1).astype(jnp.bfloat16)


def draw_w_spatial(key, part):
    return attention_weights(jax.random.fold_in(key, 101))


def draw_w_temporal(key, part):
    return attention_weights(jax.random.fold_in(key, 202))


def draw_tokens(key, part):
    base = jnp.clip(jax.random.normal(jax.random.fold_in(key, 11), (FRAMES, CELLS, D), jnp.float32), -6.0, 6.0)
    return base.astype(jnp.bfloat16)


def normal_values(own_key, shape, width, limit, kind=jnp.bfloat16):
    array = width * jax.random.normal(own_key, shape, jnp.float32)
    return jnp.clip(array, min=-limit, max=limit).astype(kind)


def setup_inputs(seed: int = 0) -> dict:
    splits = jax.random.split(jax.random.key(seed), 8)
    return {
        "tokens": draw_tokens(jax.random.fold_in(splits[7], 71), 0),
        "norm_spatial": jnp.clip(1.0 + 0.15 * jax.random.normal(splits[1], (D,), jnp.float32), 0.25, 1.75),
        "w_spatial": draw_w_spatial(jax.random.fold_in(splits[7], 71), 0),
        "w_spatial_out": normal_values(splits[3], (D, D), D ** -0.5, 0.25),
        "norm_temporal": jnp.clip(1.0 + 0.15 * jax.random.normal(splits[4], (D,), jnp.float32), 0.25, 1.75),
        "w_temporal": draw_w_temporal(jax.random.fold_in(splits[7], 71), 0),
        "w_temporal_out": normal_values(splits[6], (D, D), D ** -0.5, 0.25),
    }


def layer_norm(rows, gain):
    mean = lax.optimization_barrier(jnp.mean(rows, axis=-1, keepdims=True))
    centred = rows - mean
    spread = lax.optimization_barrier(jnp.mean(centred * centred, axis=-1, keepdims=True))
    return centred * lax.rsqrt(spread + 1e-05) * gain

def spatial_frame(qkv_frame):
    scale = 1.0 / HEAD ** 0.5

    def one_head(head):
        start = head * HEAD
        query = lax.dynamic_slice_in_dim(qkv_frame, start, HEAD, 1)
        keys = lax.dynamic_slice_in_dim(qkv_frame, D + start, HEAD, 1)
        values = lax.dynamic_slice_in_dim(qkv_frame, 2 * D + start, HEAD, 1)
        scores = jnp.dot(query, keys.T, preferred_element_type=jnp.float32) * scale
        peak = lax.optimization_barrier(jnp.max(scores, axis=1, keepdims=True))
        weights = jnp.exp(scores - peak)
        total = lax.optimization_barrier(jnp.sum(weights, axis=1, keepdims=True))
        return jnp.dot(weights.astype(jnp.bfloat16), values, preferred_element_type=jnp.float32) / total
    heads_out = lax.map(one_head, jnp.arange(HEADS, dtype=jnp.int32))
    return jnp.transpose(heads_out, (1, 0, 2)).reshape(CELLS, D).astype(jnp.bfloat16)

def temporal_cells(qkv):
    frames, cells = (qkv.shape[0], qkv.shape[1])
    scale = 1.0 / HEAD ** 0.5
    query = qkv[:, :, :D].astype(jnp.float32).reshape(frames, cells, HEADS, HEAD)
    keys = qkv[:, :, D:2 * D].astype(jnp.float32).reshape(frames, cells, HEADS, HEAD)
    values = qkv[:, :, 2 * D:].astype(jnp.float32).reshape(frames, cells, HEADS, HEAD)
    scores = jnp.einsum('fche,gche->chfg', query, keys) * scale
    later = jnp.arange(frames)[:, None] >= jnp.arange(frames)[None, :]
    scores = jnp.where(later, scores, -1e+30)
    peak = lax.optimization_barrier(jnp.max(scores, axis=3, keepdims=True))
    weights = jnp.exp(scores - peak)
    total = lax.optimization_barrier(jnp.sum(weights, axis=3))
    rounded = lax.optimization_barrier(weights.astype(jnp.bfloat16)).astype(jnp.float32)
    summed = jnp.einsum('chfg,gche->fche', rounded, values)
    context = summed / jnp.transpose(total, (2, 0, 1))[..., None]
    return context.reshape(frames, cells, D).astype(jnp.bfloat16)

def reference(tokens, norm_spatial, w_spatial, w_spatial_out, norm_temporal, w_temporal, w_temporal_out):
    resid = tokens.astype(jnp.float32)
    normed = layer_norm(resid, norm_spatial).astype(jnp.bfloat16)

    def frame_step(rows):
        qkv = jnp.dot(rows, w_spatial, preferred_element_type=jnp.float32).astype(jnp.bfloat16)
        return spatial_frame(qkv)
    context = lax.map(frame_step, normed)
    spatial = jnp.dot(context.reshape(FRAMES * CELLS, D), w_spatial_out, preferred_element_type=jnp.float32)
    after = resid + spatial.reshape(FRAMES, CELLS, D)
    second = layer_norm(after, norm_temporal).astype(jnp.bfloat16)
    qkv_t = jnp.dot(second.reshape(FRAMES * CELLS, D), w_temporal, preferred_element_type=jnp.float32)
    qkv_t = qkv_t.astype(jnp.bfloat16).reshape(FRAMES, CELLS, 3 * D)
    context_t = temporal_cells(qkv_t)
    temporal = jnp.dot(context_t.reshape(FRAMES * CELLS, D), w_temporal_out, preferred_element_type=jnp.float32)
    return (after + temporal.reshape(FRAMES, CELLS, D)).astype(jnp.bfloat16)
```

```python
import functools
import math

import jax
import jax.numpy as jnp
from jax import lax
from jax.experimental import pallas as pl
from jax.experimental.pallas import tpu as pltpu
from jax.sharding import PartitionSpec as P

HEADS = 8
HEAD = 64
GROUP = 4
HALVES = 2
FACTOR = math.log2(math.e) / math.sqrt(HEAD)
MESH = pl.DeviceIdType.MESH


def layer_norm(rows, gain):
    mean = jnp.mean(rows, axis=-1, keepdims=True)
    centred = rows - mean
    spread = jnp.mean(centred * centred, axis=-1, keepdims=True)
    return centred * lax.rsqrt(spread + 1e-05) * gain


def dot(a, b):
    return jnp.dot(a, b, preferred_element_type=jnp.float32)


def dot_t(a, b):
    return lax.dot_general(a, b, (((1,), (1,)), ((), ())), preferred_element_type=jnp.float32)


def own_lanes(shape, head):
    return lax.div(lax.broadcasted_iota(jnp.int32, shape, 1), jnp.int32(HEAD)) == head


def stack_heads(query):
    wide = query.astype(jnp.float32)
    parts = [jnp.where(own_lanes(query.shape, h), wide, 0.0) for h in range(GROUP)]
    return jnp.concatenate(parts, axis=0).astype(jnp.bfloat16)


def unstack_heads(stacked):
    n = stacked.shape[0] // GROUP
    result = stacked[:n]
    for h in range(1, GROUP):
        part = stacked[h * n : (h + 1) * n]
        result = jnp.where(own_lanes(part.shape, h), part, result)
    return result


def loop(low, high, body):
    if high - low <= 1:
        for i in range(low, high):
            body(i)
    else:
        lax.fori_loop(low, high, lambda i, c: (body(i), c)[1], 0)


def rows_of(block):
    owners, share, width = block.shape
    if share % 16:
        block = block.astype(jnp.float32)
    return block.reshape(owners * share, width).astype(jnp.bfloat16)


def kernel(
    frames, chips, chunks,
    tokens, gain_s, w_s_in, w_so_in, gain_t, w_t_in, w_to_in,
    out,
    own, w_s, w_so, w_t, w_to, land, kv, qs, acc, peak, total, after,
    sec_out, sec_in, ctx_out, ctx_in,
    load_sem, peer_send, sib_send, land_recv, sec_send, sec_recv, ctx_send, ctx_recv,
):
    rows, width = own.shape
    half = rows // HALVES
    chunk = rows // chunks
    share = chunk // frames
    group = GROUP * HEAD
    groups = width // group
    frame = lax.axis_index("frame")
    row = lax.axis_index("row")
    core = lax.rem(row, 2)
    chip = lax.div(row, 2)
    sibling = row + 1 - 2 * core

    def chip_peer(d):
        return lax.rem(chip + d, chips) * 2 + core

    def frame_peer(d):
        return lax.rem(frame + d, frames)

    loads = [
        pltpu.make_async_copy(src, dst, load_sem.at[i])
        for i, (src, dst) in enumerate(
            [(tokens, own), (w_s_in, w_s), (w_so_in, w_so), (w_t_in, w_t), (w_to_in, w_to)]
        )
    ]
    for load in loads:
        load.start()

    barrier = pltpu.get_barrier_semaphore()

    def greet(device):
        pl.semaphore_signal(barrier, inc=1, device_id=device, device_id_type=MESH)

    greet({"row": sibling})
    loop(1, chips, lambda d: greet({"row": chip_peer(d)}))
    loop(1, frames, lambda d: greet({"frame": frame_peer(d)}))
    pl.semaphore_wait(barrier, 1 + (chips - 1) + (frames - 1))

    def to_peer(d, h):
        part = pl.ds(h * half, half)
        slot = 2 * (chips - d)
        return pltpu.make_async_remote_copy(
            src_ref=tokens.at[part], dst_ref=land.at[slot, part],
            send_sem=peer_send.at[d, h], recv_sem=land_recv.at[slot, h],
            device_id={"row": chip_peer(d)}, device_id_type=MESH,
        )

    def to_sibling(j, h):
        part = pl.ds(h * half, half)
        slot = 2 * j + 1
        src = tokens.at[part] if isinstance(j, int) and j == 0 else land.at[2 * j, part]
        return pltpu.make_async_remote_copy(
            src_ref=src, dst_ref=land.at[slot, part],
            send_sem=sib_send.at[j, h], recv_sem=land_recv.at[slot, h],
            device_id={"row": sibling}, device_id_type=MESH,
        )

    for h in range(HALVES):
        loop(1, chips, lambda d: to_peer(d, h).start())
    for h in range(HALVES):
        to_sibling(0, h).start()

    def keys_values(tokens_in, place):
        normed = layer_norm(tokens_in.astype(jnp.float32), gain_s[...]).astype(jnp.bfloat16)
        n = normed.shape[0]
        kv[pl.ds(place, n), :] = dot(normed, w_s[:, width:]).astype(jnp.bfloat16)
        return normed

    loads[0].wait()
    loads[1].wait()
    normed = keys_values(own[...], 0)
    query = dot(normed, w_s[:, :width]).astype(jnp.bfloat16)
    for c in range(chunks):
        for g in range(groups):
            qs[c, g] = stack_heads(query[c * chunk : (c + 1) * chunk, g * group : (g + 1) * group])
    for h in range(HALVES):
        to_sibling(0, h).wait_recv()
    keys_values(land[1], rows)

    def attend(c, j, first):
        place = j * (2 * rows)
        if not isinstance(j, int):
            place = pl.multiple_of(place, 2 * rows)
        for g in range(groups):
            keys = kv[pl.ds(place, 2 * rows), g * group : (g + 1) * group]
            values = kv[pl.ds(place, 2 * rows), width + g * group : width + (g + 1) * group]
            scores = dot_t(qs[c, g], keys)
            high = jnp.max(scores, axis=1, keepdims=True)
            if not first:
                before = peak[c, g][:, :1]
                high = jnp.maximum(before, high)
                fade = jnp.exp2((before - high) * FACTOR)
            weights = jnp.exp2((scores - high) * FACTOR)
            added = jnp.sum(weights, axis=1, keepdims=True)
            product = dot(weights.astype(jnp.bfloat16), values)
            if first:
                acc[c, g] = product
            else:
                added = added + total[c, g][:, :1] * fade
                acc[c, g] = acc[c, g] * fade + product
            peak[c, g] = jnp.broadcast_to(high, peak.shape[2:])
            total[c, g] = jnp.broadcast_to(added, total.shape[2:])

    for c in range(chunks):
        attend(c, 0, True)

    def take(j):
        for h in range(HALVES):
            to_peer(chips - j, h).wait_recv()
            to_sibling(j, h).start()
            keys_values(land[2 * j, pl.ds(h * half, half)], 2 * j * rows + h * half)
        for h in range(HALVES):
            to_sibling(j, h).wait_recv()
            keys_values(land[2 * j + 1, pl.ds(h * half, half)], (2 * j + 1) * rows + h * half)

    loop(1, chips, take)
    loads[2].wait()

    def exchange(c, d, src, dst, send, recv):
        peer = frame_peer(d)
        return pltpu.make_async_remote_copy(
            src_ref=src.at[c, peer], dst_ref=dst.at[c, frame],
            send_sem=send.at[c, d], recv_sem=recv.at[c, frames - d],
            device_id={"frame": peer}, device_id_type=MESH,
        )

    def second_copy(c, d):
        return exchange(c, d, sec_out, sec_in, sec_send, sec_recv)

    def context_copy(c, d):
        return exchange(c, d, ctx_out, ctx_in, ctx_send, ctx_recv)

    for c in range(chunks):
        loop(1, chips, lambda j: attend(c, j, False))
        parts = [unstack_heads(acc[c, g] / total[c, g][:, :1]) for g in range(groups)]
        context = jnp.concatenate(parts, axis=1).astype(jnp.bfloat16)
        here = slice(c * chunk, (c + 1) * chunk)
        rest = own[here].astype(jnp.float32) + dot(context, w_so[...])
        after[here] = rest
        second = layer_norm(rest, gain_t[...]).reshape(frames, share, width).astype(jnp.bfloat16)
        sec_out[c] = second
        loop(1, frames, lambda d: second_copy(c, d).start())
        sec_in[c, frame] = sec_out[c, frame]

    loads[3].wait()
    shape = (GROUP * chunk, chunk)
    q_place = lax.rem(lax.broadcasted_iota(jnp.int32, shape, 0), jnp.int32(chunk))
    k_place = lax.broadcasted_iota(jnp.int32, shape, 1)
    seen = (lax.rem(q_place, jnp.int32(share)) == lax.rem(k_place, jnp.int32(share))) & (
        k_place <= q_place
    )
    for c in range(chunks):
        loop(1, frames, lambda d: second_copy(c, d).wait_recv())
        qkv = dot(rows_of(sec_in[c]), w_t[...]).astype(jnp.bfloat16)
        parts = []
        for g in range(groups):
            query = stack_heads(qkv[:, g * group : (g + 1) * group])
            keys = qkv[:, width + g * group : width + (g + 1) * group]
            values = qkv[:, 2 * width + g * group : 2 * width + (g + 1) * group]
            scores = jnp.where(seen, dot_t(query, keys), -1e30)
            high = jnp.max(scores, axis=1, keepdims=True)
            weights = jnp.exp2((scores - high) * FACTOR)
            added = jnp.sum(weights, axis=1, keepdims=True)
            parts.append(unstack_heads(dot(weights.astype(jnp.bfloat16), values) / added))
        context = jnp.concatenate(parts, axis=1).reshape(frames, share, width)
        ctx_out[c] = context.astype(jnp.bfloat16)
        loop(1, frames, lambda d: context_copy(c, d).start())
        ctx_in[c, frame] = ctx_out[c, frame]

    loads[4].wait()
    for c in range(chunks):
        loop(1, frames, lambda d: context_copy(c, d).wait_recv())
        here = slice(c * chunk, (c + 1) * chunk)
        out[here] = (after[here] + dot(rows_of(ctx_in[c]), w_to[...])).astype(out.dtype)

    for h in range(HALVES):
        loop(1, chips, lambda d: to_peer(d, h).wait_send())
        to_sibling(0, h).wait_send()
        loop(1, chips, lambda j: to_sibling(j, h).wait_send())
    for c in range(chunks):
        loop(1, frames, lambda d: second_copy(c, d).wait_send())
        loop(1, frames, lambda d: context_copy(c, d).wait_send())


def shards(tokens, gain_s, w_s, w_so, gain_t, w_t, w_to):
    _, rows, width = tokens.shape
    frames = lax.axis_size("frame")
    peers = lax.axis_size("row")
    chips = peers // 2
    chunks = 2 if rows // frames % 32 == 0 else 1
    chunk = rows // chunks
    share = chunk // frames
    group = GROUP * HEAD
    groups = width // group
    bf16, f32 = jnp.bfloat16, jnp.float32
    vmem = pl.BlockSpec(memory_space=pltpu.VMEM)
    hbm = pl.BlockSpec(memory_space=pl.ANY)
    dma = pltpu.SemaphoreType.DMA
    mixed = pl.pallas_call(
        functools.partial(kernel, frames, chips, chunks),
        out_shape=jax.ShapeDtypeStruct((rows, width), bf16),
        in_specs=[hbm, vmem, hbm, hbm, vmem, hbm, hbm],
        out_specs=vmem,
        scratch_shapes=[
            pltpu.VMEM((rows, width), bf16),
            pltpu.VMEM(w_s.shape, bf16),
            pltpu.VMEM(w_so.shape, bf16),
            pltpu.VMEM(w_t.shape, bf16),
            pltpu.VMEM(w_to.shape, bf16),
            pltpu.VMEM((peers, rows, width), bf16),
            pltpu.VMEM((peers * rows, 2 * width), bf16),
            pltpu.VMEM((chunks, groups, GROUP * chunk, group), bf16),
            pltpu.VMEM((chunks, groups, GROUP * chunk, group), f32),
            pltpu.VMEM((chunks, groups, GROUP * chunk, 128), f32),
            pltpu.VMEM((chunks, groups, GROUP * chunk, 128), f32),
            pltpu.VMEM((rows, width), f32),
            pltpu.VMEM((chunks, frames, share, width), bf16),
            pltpu.VMEM((chunks, frames, share, width), bf16),
            pltpu.VMEM((chunks, frames, share, width), bf16),
            pltpu.VMEM((chunks, frames, share, width), bf16),
            dma((5,)),
            dma((chips, HALVES)),
            dma((chips, HALVES)),
            dma((peers, HALVES)),
            dma((chunks, frames)),
            dma((chunks, frames)),
            dma((chunks, frames)),
            dma((chunks, frames)),
        ],
        compiler_params=pltpu.CompilerParams(
            collective_id=0, has_side_effects=True, vmem_limit_bytes=52 * 1024 * 1024
        ),
        cost_estimate=pl.CostEstimate(
            flops=6_000_000_000, bytes_accessed=8_000_000, transcendentals=4_000_000
        ),
    )(tokens.reshape(rows, width), gain_s.reshape(1, width), w_s, w_so, gain_t.reshape(1, width), w_t, w_to)
    return mixed.reshape(1, rows, width)


def solution(mesh):
    in_specs = (P("frame", "row", None), P(), P(), P(), P(), P(), P())
    out_specs = P("frame", "row", None)
    return jax.shard_map(shards, mesh=mesh, in_specs=in_specs, out_specs=out_specs, check_vma=False)
```

```python
import functools
import math

import jax
import jax.numpy as jnp
from jax import lax
from jax.experimental import pallas as pl
from jax.experimental.pallas import tpu as pltpu
from jax.sharding import PartitionSpec as P

HEADS = 8
HEAD = 64
LANES = 128
GROUP = 4
HALVES = 2
FACTOR = math.log2(math.e) / math.sqrt(HEAD)
MESH = pl.DeviceIdType.MESH


def layer_norm(rows, gain):
    mean = jnp.mean(rows, axis=-1, keepdims=True)
    centred = rows - mean
    spread = jnp.mean(centred * centred, axis=-1, keepdims=True)
    return centred * lax.rsqrt(spread + 1e-05) * gain


def dot(a, b):
    return jnp.dot(a, b, preferred_element_type=jnp.float32)


def dot_t(a, b):
    return lax.dot_general(a, b, (((1,), (1,)), ((), ())), preferred_element_type=jnp.float32)


def own_lanes(shape, head):
    return lax.div(lax.broadcasted_iota(jnp.int32, shape, 1), jnp.int32(HEAD)) == head


def stack_heads(query):
    wide = query.astype(jnp.float32)
    parts = [jnp.where(own_lanes(query.shape, h), wide, 0.0) for h in range(GROUP)]
    return jnp.concatenate(parts, axis=0).astype(jnp.bfloat16)


def unstack_heads(stacked):
    n = stacked.shape[0] // GROUP
    result = stacked[:n]
    for h in range(1, GROUP):
        part = stacked[h * n : (h + 1) * n]
        result = jnp.where(own_lanes(part.shape, h), part, result)
    return result


def loop(low, high, body):
    if high - low <= 8:
        for i in range(low, high):
            body(i)
    else:
        lax.fori_loop(low, high, lambda i, c: (body(i), c)[1], 0)


def rows_of(block):
    owners, share, width = block.shape
    if share % 16:
        block = block.astype(jnp.float32)
    return block.reshape(owners * share, width).astype(jnp.bfloat16)


def kernel(
    frames, chips, chunks,
    tokens, gain_s, w_s_in, w_so_in, gain_t, w_t_in, w_to_in,
    out,
    own, w_s, w_so, w_t, w_to, land, kv, qs, acc, peak, total, after,
    sec_out, sec_in, ctx_out, ctx_in,
    load_sem, peer_send, sib_send, land_recv, sec_send, sec_recv, ctx_send, ctx_recv,
):
    rows, width = own.shape
    half = rows // HALVES
    chunk = rows // chunks
    share = chunk // frames
    group = GROUP * HEAD
    groups = width // group
    frame = lax.axis_index("frame")
    row = lax.axis_index("row")
    core = lax.rem(row, 2)
    chip = lax.div(row, 2)
    sibling = row + 1 - 2 * core

    def chip_peer(d):
        return lax.rem(chip + d, chips) * 2 + core

    def frame_peer(d):
        return lax.rem(frame + d, frames)

    loads = [
        pltpu.make_async_copy(src, dst, load_sem.at[i])
        for i, (src, dst) in enumerate(
            [(tokens, own), (w_s_in, w_s), (w_so_in, w_so), (w_t_in, w_t), (w_to_in, w_to)]
        )
    ]
    for load in loads:
        load.start()

    barrier = pltpu.get_barrier_semaphore()

    def greet(device):
        pl.semaphore_signal(barrier, inc=1, device_id=device, device_id_type=MESH)

    greet({"row": sibling})
    loop(1, chips, lambda d: greet({"row": chip_peer(d)}))
    loop(1, frames, lambda d: greet({"frame": frame_peer(d)}))
    pl.semaphore_wait(barrier, 1 + (chips - 1) + (frames - 1))

    def to_peer(d, h):
        part = pl.ds(h * half, half)
        slot = 2 * (chips - d)
        return pltpu.make_async_remote_copy(
            src_ref=tokens.at[part], dst_ref=land.at[slot, part],
            send_sem=peer_send.at[d, h], recv_sem=land_recv.at[slot, h],
            device_id={"row": chip_peer(d)}, device_id_type=MESH,
        )

    def to_sibling(j, h):
        part = pl.ds(h * half, half)
        slot = 2 * j + 1
        src = tokens.at[part] if isinstance(j, int) and j == 0 else land.at[2 * j, part]
        return pltpu.make_async_remote_copy(
            src_ref=src, dst_ref=land.at[slot, part],
            send_sem=sib_send.at[j, h], recv_sem=land_recv.at[slot, h],
            device_id={"row": sibling}, device_id_type=MESH,
        )

    for h in range(HALVES):
        loop(1, chips, lambda d: to_peer(d, h).start())
    for h in range(HALVES):
        to_sibling(0, h).start()

    def keys_values(tokens_in, place):
        normed = layer_norm(tokens_in.astype(jnp.float32), gain_s[...]).astype(jnp.bfloat16)
        n = normed.shape[0]
        kv[pl.ds(place, n), :] = dot(normed, w_s[:, width:]).astype(jnp.bfloat16)
        return normed

    loads[0].wait()
    loads[1].wait()
    normed = keys_values(own[...], 0)
    query = dot(normed, w_s[:, :width]).astype(jnp.bfloat16)
    for c in range(chunks):
        for g in range(groups):
            qs[c, g] = stack_heads(query[c * chunk : (c + 1) * chunk, g * group : (g + 1) * group])
    for h in range(HALVES):
        to_sibling(0, h).wait_recv()
    keys_values(land[1], rows)

    def attend(c, place, count, first=False):
        if not isinstance(place, int):
            place = pl.multiple_of(place, count)
        for g in range(groups):
            keys = kv[pl.ds(place, count), g * group : (g + 1) * group]
            values = kv[pl.ds(place, count), width + g * group : width + (g + 1) * group]
            scores = dot_t(qs[c, g], keys)
            high = jnp.max(scores, axis=1, keepdims=True)
            if not first:
                before = peak[c, g]
                high = jnp.maximum(before[:, :1], high)
            weights = jnp.exp2((scores - high) * FACTOR)
            added = sum(weights[:, i : i + LANES] for i in range(0, count, LANES))
            product = dot(weights.astype(jnp.bfloat16), values)
            high = jnp.broadcast_to(high, peak.shape[2:])
            if first:
                acc[c, g] = product
                total[c, g] = added
            else:
                fade = jnp.exp2((before - high) * FACTOR)
                total[c, g] = total[c, g] * fade + added
                acc[c, g] = acc[c, g] * jnp.concatenate([fade] * (group // LANES), 1) + product
            peak[c, g] = high

    for c in range(chunks):
        attend(c, 0, 2 * rows, True)

    def place_of(j, h):
        return 2 * j * rows + h * 2 * half

    def take(j, h):
        part = pl.ds(h * half, half)
        to_peer(chips - j, h).wait_recv()
        to_sibling(j, h).start()
        keys_values(land[2 * j, part], place_of(j, h))
        to_sibling(j, h).wait_recv()
        keys_values(land[2 * j + 1, part], place_of(j, h) + half)

    def take_and_attend(j, h):
        take(j, h)
        for c in range(chunks):
            attend(c, place_of(j, h), 2 * half)

    last = HALVES - 1
    for h in range(last):
        loop(1, chips, lambda j: take_and_attend(j, h))
    loop(1, chips, lambda j: take(j, last))
    loads[2].wait()

    def exchange(c, d, src, dst, send, recv):
        peer = frame_peer(d)
        return pltpu.make_async_remote_copy(
            src_ref=src.at[c, peer], dst_ref=dst.at[c, frame],
            send_sem=send.at[c, d], recv_sem=recv.at[c, frames - d],
            device_id={"frame": peer}, device_id_type=MESH,
        )

    def far_first(i):
        return frames // 2 + (i // 2) * (1 - 2 * (i % 2))

    def second_copy(c, d):
        return exchange(c, d, sec_out, sec_in, sec_send, sec_recv)

    def context_copy(c, d):
        return exchange(c, d, ctx_out, ctx_in, ctx_send, ctx_recv)

    for c in range(chunks):
        loop(1, chips, lambda j: attend(c, place_of(j, last), 2 * half))
        parts = [
            unstack_heads(acc[c, g] / jnp.sum(total[c, g], axis=1, keepdims=True))
            for g in range(groups)
        ]
        context = jnp.concatenate(parts, axis=1).astype(jnp.bfloat16)
        here = slice(c * chunk, (c + 1) * chunk)
        rest = own[here].astype(jnp.float32) + dot(context, w_so[...])
        after[here] = rest
        second = layer_norm(rest, gain_t[...]).reshape(frames, share, width).astype(jnp.bfloat16)
        sec_out[c] = second
        loop(1, frames, lambda i: second_copy(c, far_first(i)).start())
        sec_in[c, frame] = sec_out[c, frame]

    loads[3].wait()
    shape = (GROUP * chunk, chunk)
    q_place = lax.rem(lax.broadcasted_iota(jnp.int32, shape, 0), jnp.int32(chunk))
    k_place = lax.broadcasted_iota(jnp.int32, shape, 1)
    seen = (lax.rem(q_place, jnp.int32(share)) == lax.rem(k_place, jnp.int32(share))) & (
        k_place <= q_place
    )
    for c in range(chunks):
        loop(1, frames, lambda d: second_copy(c, d).wait_recv())
        qkv = dot(rows_of(sec_in[c]), w_t[...]).astype(jnp.bfloat16)
        parts = []
        for g in range(groups):
            query = stack_heads(qkv[:, g * group : (g + 1) * group])
            keys = qkv[:, width + g * group : width + (g + 1) * group]
            values = qkv[:, 2 * width + g * group : 2 * width + (g + 1) * group]
            scores = jnp.where(seen, dot_t(query, keys), -1e30)
            high = jnp.max(scores, axis=1, keepdims=True)
            weights = jnp.exp2((scores - high) * FACTOR)
            added = jnp.sum(weights, axis=1, keepdims=True)
            parts.append(unstack_heads(dot(weights.astype(jnp.bfloat16), values) / added))
        context = jnp.concatenate(parts, axis=1).reshape(frames, share, width)
        ctx_out[c] = context.astype(jnp.bfloat16)
        loop(1, frames, lambda i: context_copy(c, far_first(i)).start())
        ctx_in[c, frame] = ctx_out[c, frame]

    loads[4].wait()
    for c in range(chunks):
        loop(1, frames, lambda d: context_copy(c, d).wait_recv())
        here = slice(c * chunk, (c + 1) * chunk)
        out[here] = (after[here] + dot(rows_of(ctx_in[c]), w_to[...])).astype(out.dtype)

    for h in range(HALVES):
        loop(1, chips, lambda d: to_peer(d, h).wait_send())
        to_sibling(0, h).wait_send()
        loop(1, chips, lambda j: to_sibling(j, h).wait_send())
    for c in range(chunks):
        loop(1, frames, lambda d: second_copy(c, d).wait_send())
        loop(1, frames, lambda d: context_copy(c, d).wait_send())


def shards(tokens, gain_s, w_s, w_so, gain_t, w_t, w_to):
    _, rows, width = tokens.shape
    frames = lax.axis_size("frame")
    peers = lax.axis_size("row")
    chips = peers // 2
    chunks = 2 if rows // frames % 32 == 0 else 1
    chunk = rows // chunks
    share = chunk // frames
    group = GROUP * HEAD
    groups = width // group
    bf16, f32 = jnp.bfloat16, jnp.float32
    vmem = pl.BlockSpec(memory_space=pltpu.VMEM)
    hbm = pl.BlockSpec(memory_space=pl.ANY)
    dma = pltpu.SemaphoreType.DMA
    mixed = pl.pallas_call(
        functools.partial(kernel, frames, chips, chunks),
        out_shape=jax.ShapeDtypeStruct((rows, width), bf16),
        in_specs=[hbm, vmem, hbm, hbm, vmem, hbm, hbm],
        out_specs=vmem,
        scratch_shapes=[
            pltpu.VMEM((rows, width), bf16),
            pltpu.VMEM(w_s.shape, bf16),
            pltpu.VMEM(w_so.shape, bf16),
            pltpu.VMEM(w_t.shape, bf16),
            pltpu.VMEM(w_to.shape, bf16),
            pltpu.VMEM((peers, rows, width), bf16),
            pltpu.VMEM((peers * rows, 2 * width), bf16),
            pltpu.VMEM((chunks, groups, GROUP * chunk, group), bf16),
            pltpu.VMEM((chunks, groups, GROUP * chunk, group), f32),
            pltpu.VMEM((chunks, groups, GROUP * chunk, LANES), f32),
            pltpu.VMEM((chunks, groups, GROUP * chunk, LANES), f32),
            pltpu.VMEM((rows, width), f32),
            pltpu.VMEM((chunks, frames, share, width), bf16),
            pltpu.VMEM((chunks, frames, share, width), bf16),
            pltpu.VMEM((chunks, frames, share, width), bf16),
            pltpu.VMEM((chunks, frames, share, width), bf16),
            dma((5,)),
            dma((chips, HALVES)),
            dma((chips, HALVES)),
            dma((peers, HALVES)),
            dma((chunks, frames)),
            dma((chunks, frames)),
            dma((chunks, frames)),
            dma((chunks, frames)),
        ],
        compiler_params=pltpu.CompilerParams(
            collective_id=0, has_side_effects=True, vmem_limit_bytes=64 * 1024 * 1024
        ),
        cost_estimate=pl.CostEstimate(
            flops=6_000_000_000, bytes_accessed=8_000_000, transcendentals=4_000_000
        ),
    )(tokens.reshape(rows, width), gain_s.reshape(1, width), w_s, w_so, gain_t.reshape(1, width), w_t, w_to)
    return mixed.reshape(1, rows, width)


def solution(mesh):
    in_specs = (P("frame", "row", None), P(), P(), P(), P(), P(), P())
    out_specs = P("frame", "row", None)
    return jax.shard_map(shards, mesh=mesh, in_specs=in_specs, out_specs=out_specs, check_vma=False)
```

```python
import functools
import math

import jax
import jax.numpy as jnp
from jax import lax
from jax.experimental import pallas as pl
from jax.experimental.pallas import tpu as pltpu
from jax.sharding import PartitionSpec as P

HEADS = 8
HEAD = 64
LANES = 128
GROUP = 4
HALVES = 2
FACTOR = math.log2(math.e) / math.sqrt(HEAD)
MESH = pl.DeviceIdType.MESH


def layer_norm(rows, gain):
    mean = jnp.mean(rows, axis=-1, keepdims=True)
    centred = rows - mean
    spread = jnp.mean(centred * centred, axis=-1, keepdims=True)
    return centred * lax.rsqrt(spread + 1e-05) * gain


def dot(a, b):
    return jnp.dot(a, b, preferred_element_type=jnp.float32)


def dot_t(a, b):
    return lax.dot_general(a, b, (((1,), (1,)), ((), ())), preferred_element_type=jnp.float32)


def own_lanes(shape, head):
    return lax.div(lax.broadcasted_iota(jnp.int32, shape, 1), jnp.int32(HEAD)) == head


def stack_heads(query):
    wide = query.astype(jnp.float32)
    parts = [jnp.where(own_lanes(query.shape, h), wide, 0.0) for h in range(GROUP)]
    return jnp.concatenate(parts, axis=0).astype(jnp.bfloat16)


def unstack_heads(stacked):
    n = stacked.shape[0] // GROUP
    result = stacked[:n]
    for h in range(1, GROUP):
        part = stacked[h * n : (h + 1) * n]
        result = jnp.where(own_lanes(part.shape, h), part, result)
    return result


def loop(low, high, body):
    if high - low <= 8:
        for i in range(low, high):
            body(i)
    else:
        lax.fori_loop(low, high, lambda i, c: (body(i), c)[1], 0)


def rows_of(block):
    owners, share, width = block.shape
    if share % 16:
        block = block.astype(jnp.float32)
    return block.reshape(owners * share, width).astype(jnp.bfloat16)


def kernel(
    frames, chips, chunks,
    tokens, gain_s, w_s_in, w_so_in, gain_t, w_t_in, w_to_in,
    out,
    own, w_s, w_so, w_t, w_to, land, kv, qs, acc, peak, total, after,
    sec_out, sec_in, ctx_out, ctx_in,
    load_sem, peer_send, sib_send, land_recv, sec_send, sec_recv, ctx_send, ctx_recv,
):
    rows, width = own.shape
    half = rows // HALVES
    chunk = rows // chunks
    share = chunk // frames
    group = GROUP * HEAD
    groups = width // group
    frame = lax.axis_index("frame")
    row = lax.axis_index("row")
    core = lax.rem(row, 2)
    chip = lax.div(row, 2)
    sibling = row + 1 - 2 * core

    def chip_peer(d):
        return lax.rem(chip + d, chips) * 2 + core

    def frame_peer(d):
        return lax.rem(frame + d, frames)

    loads = [
        pltpu.make_async_copy(src, dst, load_sem.at[i])
        for i, (src, dst) in enumerate(
            [(tokens, own), (w_s_in, w_s), (w_so_in, w_so), (w_t_in, w_t), (w_to_in, w_to)]
        )
    ]
    for load in loads:
        load.start()

    barrier = pltpu.get_barrier_semaphore()

    def greet(device):
        pl.semaphore_signal(barrier, inc=1, device_id=device, device_id_type=MESH)

    greet({"row": sibling})
    loop(1, chips, lambda d: greet({"row": chip_peer(d)}))
    loop(1, frames, lambda d: greet({"frame": frame_peer(d)}))
    pl.semaphore_wait(barrier, 1 + (chips - 1) + (frames - 1))

    def to_peer(d, h):
        part = pl.ds(h * half, half)
        slot = 2 * (chips - d)
        return pltpu.make_async_remote_copy(
            src_ref=tokens.at[part], dst_ref=land.at[slot, part],
            send_sem=peer_send.at[d, h], recv_sem=land_recv.at[slot, h],
            device_id={"row": chip_peer(d)}, device_id_type=MESH,
        )

    def to_sibling(j, h):
        part = pl.ds(h * half, half)
        slot = 2 * j + 1
        src = tokens.at[part] if isinstance(j, int) and j == 0 else land.at[2 * j, part]
        return pltpu.make_async_remote_copy(
            src_ref=src, dst_ref=land.at[slot, part],
            send_sem=sib_send.at[j, h], recv_sem=land_recv.at[slot, h],
            device_id={"row": sibling}, device_id_type=MESH,
        )

    for h in range(HALVES):
        loop(1, chips, lambda d: to_peer(d, h).start())
    for h in range(HALVES):
        to_sibling(0, h).start()

    def keys_values(tokens_in, place):
        normed = layer_norm(tokens_in.astype(jnp.float32), gain_s[...]).astype(jnp.bfloat16)
        n = normed.shape[0]
        kv[pl.ds(place, n), :] = dot(normed, w_s[:, width:]).astype(jnp.bfloat16)
        return normed

    loads[0].wait()
    loads[1].wait()
    normed = keys_values(own[...], 0)
    query = dot(normed, w_s[:, :width]).astype(jnp.bfloat16)
    for c in range(chunks):
        for g in range(groups):
            qs[c, g] = stack_heads(query[c * chunk : (c + 1) * chunk, g * group : (g + 1) * group])
    for h in range(HALVES):
        to_sibling(0, h).wait_recv()
    keys_values(land[1], rows)

    def attend(c, place, count, first=False):
        if not isinstance(place, int):
            place = pl.multiple_of(place, count)
        for g in range(groups):
            keys = kv[pl.ds(place, count), g * group : (g + 1) * group]
            values = kv[pl.ds(place, count), width + g * group : width + (g + 1) * group]
            scores = dot_t(qs[c, g], keys)
            high = jnp.max(scores, axis=1, keepdims=True)
            if not first:
                before = peak[c, g]
                high = jnp.maximum(before[:, :1], high)
            weights = jnp.exp2((scores - high) * FACTOR)
            added = sum(weights[:, i : i + LANES] for i in range(0, count, LANES))
            product = dot(weights.astype(jnp.bfloat16), values)
            high = jnp.broadcast_to(high, peak.shape[2:])
            if first:
                acc[c, g] = product
                total[c, g] = added
            else:
                fade = jnp.exp2((before - high) * FACTOR)
                total[c, g] = total[c, g] * fade + added
                acc[c, g] = acc[c, g] * jnp.concatenate([fade] * (group // LANES), 1) + product
            peak[c, g] = high

    for c in range(chunks):
        attend(c, 0, 2 * rows, True)

    def place_of(j, h):
        return 2 * j * rows + h * 2 * half

    def take(j, h):
        part = pl.ds(h * half, half)
        to_peer(chips - j, h).wait_recv()
        to_sibling(j, h).start()
        keys_values(land[2 * j, part], place_of(j, h))
        to_sibling(j, h).wait_recv()
        keys_values(land[2 * j + 1, part], place_of(j, h) + half)

    def take_and_attend(j, h):
        take(j, h)
        for c in range(chunks):
            attend(c, place_of(j, h), 2 * half)

    last = HALVES - 1
    for h in range(last):
        loop(1, chips, lambda j: take_and_attend(j, h))
    loop(1, chips, lambda j: take(j, last))
    loads[2].wait()

    def exchange(c, d, src, dst, send, recv):
        peer = frame_peer(d)
        return pltpu.make_async_remote_copy(
            src_ref=src.at[c, peer], dst_ref=dst.at[c, frame],
            send_sem=send.at[c, d], recv_sem=recv.at[c, frames - d],
            device_id={"frame": peer}, device_id_type=MESH,
        )

    def far_first(i):
        return frames // 2 + (i // 2) * (1 - 2 * (i % 2))

    def second_copy(c, d):
        return exchange(c, d, sec_out, sec_in, sec_send, sec_recv)

    def context_copy(c, d):
        return exchange(c, d, ctx_out, ctx_in, ctx_send, ctx_recv)

    for c in range(chunks):
        loop(1, chips, lambda j: attend(c, place_of(j, last), 2 * half))
        parts = [
            unstack_heads(acc[c, g] * (1.0 / jnp.sum(total[c, g], axis=1, keepdims=True)))
            for g in range(groups)
        ]
        context = jnp.concatenate(parts, axis=1).astype(jnp.bfloat16)
        here = slice(c * chunk, (c + 1) * chunk)
        rest = own[here].astype(jnp.float32) + dot(context, w_so[...])
        after[here] = rest
        second = layer_norm(rest, gain_t[...]).reshape(frames, share, width).astype(jnp.bfloat16)
        sec_out[c] = second
        loop(1, frames, lambda i: second_copy(c, far_first(i)).start())
        sec_in[c, frame] = sec_out[c, frame]

    loads[3].wait()
    shape = (GROUP * chunk, chunk)
    q_place = lax.rem(lax.broadcasted_iota(jnp.int32, shape, 0), jnp.int32(chunk))
    k_place = lax.broadcasted_iota(jnp.int32, shape, 1)
    seen = (lax.rem(q_place, jnp.int32(share)) == lax.rem(k_place, jnp.int32(share))) & (
        k_place <= q_place
    )
    for c in range(chunks):
        loop(1, frames, lambda d: second_copy(c, d).wait_recv())
        qkv = dot(rows_of(sec_in[c]), w_t[...]).astype(jnp.bfloat16)
        parts = []
        for g in range(groups):
            query = stack_heads(qkv[:, g * group : (g + 1) * group])
            keys = qkv[:, width + g * group : width + (g + 1) * group]
            values = qkv[:, 2 * width + g * group : 2 * width + (g + 1) * group]
            scores = jnp.where(seen, dot_t(query, keys), -1e30)
            high = jnp.max(scores, axis=1, keepdims=True)
            weights = jnp.exp2((scores - high) * FACTOR)
            added = jnp.sum(weights, axis=1, keepdims=True)
            parts.append(unstack_heads(dot(weights.astype(jnp.bfloat16), values) * (1.0 / added)))
        context = jnp.concatenate(parts, axis=1).reshape(frames, share, width)
        ctx_out[c] = context.astype(jnp.bfloat16)
        loop(1, frames, lambda i: context_copy(c, far_first(i)).start())
        ctx_in[c, frame] = ctx_out[c, frame]

    loads[4].wait()
    for c in range(chunks):
        loop(1, frames, lambda d: context_copy(c, d).wait_recv())
        here = slice(c * chunk, (c + 1) * chunk)
        out[here] = (after[here] + dot(rows_of(ctx_in[c]), w_to[...])).astype(out.dtype)

    for h in range(HALVES):
        loop(1, chips, lambda d: to_peer(d, h).wait_send())
        to_sibling(0, h).wait_send()
        loop(1, chips, lambda j: to_sibling(j, h).wait_send())
    for c in range(chunks):
        loop(1, frames, lambda d: second_copy(c, d).wait_send())
        loop(1, frames, lambda d: context_copy(c, d).wait_send())


def shards(tokens, gain_s, w_s, w_so, gain_t, w_t, w_to):
    _, rows, width = tokens.shape
    frames = lax.axis_size("frame")
    peers = lax.axis_size("row")
    chips = peers // 2
    chunks = 2 if rows // frames % 32 == 0 else 1
    chunk = rows // chunks
    share = chunk // frames
    group = GROUP * HEAD
    groups = width // group
    bf16, f32 = jnp.bfloat16, jnp.float32
    vmem = pl.BlockSpec(memory_space=pltpu.VMEM)
    hbm = pl.BlockSpec(memory_space=pl.ANY)
    dma = pltpu.SemaphoreType.DMA
    mixed = pl.pallas_call(
        functools.partial(kernel, frames, chips, chunks),
        out_shape=pltpu.VMEM((rows, width), bf16),
        in_specs=[hbm, vmem, hbm, hbm, vmem, hbm, hbm],
        out_specs=vmem,
        scratch_shapes=[
            pltpu.VMEM((rows, width), bf16),
            pltpu.VMEM(w_s.shape, bf16),
            pltpu.VMEM(w_so.shape, bf16),
            pltpu.VMEM(w_t.shape, bf16),
            pltpu.VMEM(w_to.shape, bf16),
            pltpu.VMEM((peers, rows, width), bf16),
            pltpu.VMEM((peers * rows, 2 * width), bf16),
            pltpu.VMEM((chunks, groups, GROUP * chunk, group), bf16),
            pltpu.VMEM((chunks, groups, GROUP * chunk, group), f32),
            pltpu.VMEM((chunks, groups, GROUP * chunk, LANES), f32),
            pltpu.VMEM((chunks, groups, GROUP * chunk, LANES), f32),
            pltpu.VMEM((rows, width), f32),
            pltpu.VMEM((chunks, frames, share, width), bf16),
            pltpu.VMEM((chunks, frames, share, width), bf16),
            pltpu.VMEM((chunks, frames, share, width), bf16),
            pltpu.VMEM((chunks, frames, share, width), bf16),
            dma((5,)),
            dma((chips, HALVES)),
            dma((chips, HALVES)),
            dma((peers, HALVES)),
            dma((chunks, frames)),
            dma((chunks, frames)),
            dma((chunks, frames)),
            dma((chunks, frames)),
        ],
        compiler_params=pltpu.CompilerParams(
            collective_id=0, has_side_effects=True, vmem_limit_bytes=63 * 1024 * 1024
        ),
        cost_estimate=pl.CostEstimate(
            flops=6_000_000_000, bytes_accessed=8_000_000, transcendentals=4_000_000
        ),
    )(tokens.reshape(rows, width), gain_s.reshape(1, width), w_s, w_so, gain_t.reshape(1, width), w_t, w_to)
    return mixed.reshape(1, rows, width)


def solution(mesh):
    in_specs = (P("frame", "row", None), P(), P(), P(), P(), P(), P())
    out_specs = P("frame", "row", None)
    return jax.shard_map(shards, mesh=mesh, in_specs=in_specs, out_specs=out_specs, check_vma=False)
```
